32 devices in a mesh: grp: 4 (over x, core), tp: 8 (over z, y).
Axes of the slice: x: 2, y: 2, z: 4, core: 2. Of those that a mesh axis runs over, the one named last changes fastest.
Arguments:
- teacher_hidden: bfloat16 [384, 8192], P(('grp', 'tp')), may hold values from -150 to 150
- teacher_head: bfloat16 [8192, 98304], P(None, ('grp', 'tp')), may hold values from -0.0625 to 0.0625
- student_hidden: bfloat16 [384, 3584], P(('grp', 'tp')), may hold values from -150 to 150
- student_head: bfloat16 [3584, 98304], P(None, ('grp', 'tp')), may hold values from -0.09375 to 0.09375
- labels: int32 [384], replicated, may hold values from 0 to 98303
- owner_map: int32 [384], replicated, may hold values from 0 to 383, each once
Outputs:
- token_loss: float32 [384], P(('grp', 'tp'))
- grad_head: bfloat16 [3584, 98304], P(None, ('grp', 'tp'))
- grad_hidden: bfloat16 [384, 3584], P(('grp', 'tp'))
The draws below stay inside these ranges and needn't reach their ends.
Inputs may be any that keep to these rules, and one draw needn't show every extreme that they name: owner_map holds each of 0 to 383 once.
All inputs are finite; a program needn't handle non-finite values.
Results may differ from the reference program's by a relative error of at most 0.0085.
Values may be sent and summed in bfloat16 or wider, within the bound.
A program may use at most 192 MiB of HBM per device.

```python
import math
import jax
import jax.numpy as jnp
import numpy as np
from jax import lax

TEACHER_DIM = 8192
STUDENT_DIM = 3584
VOCABULARY = 98304
TOKENS = 384


def rough_rows(key, rows, cols):
    first, second = jax.random.split(key)
    values = jnp.clip(jax.random.normal(first, (rows, cols), jnp.float32), -4.0, 4.0)
    scales = jnp.exp(jax.random.uniform(second, (rows, 1), jnp.float32, math.log(1.5), math.log(6.0)))
    return values * scales


def draw_teacher_hidden(key, part):
    inner = jax.random.fold_in(key, 17)
    return rough_rows(inner, TOKENS, TEACHER_DIM).astype(jnp.bfloat16)


def draw_student_hidden(key, part):
    inner = jax.random.fold_in(key, 29)
    return rough_rows(inner, TOKENS, STUDENT_DIM).astype(jnp.bfloat16)


def with_ends(result, rng, least, largest):
    spot = [jax.random.randint(jax.random.fold_in(rng, axis), (), 0, length) for axis, length in enumerate(result.shape)]
    longest = result.shape.index(max(result.shape))
    beside = spot[:longest] + [(spot[longest] + 1) % result.shape[longest]] + spot[longest + 1:]
    return result.at[tuple(spot)].set(least).at[tuple(beside)].set(largest)


def steps_of(rng, shape, cuts, low, high):
    factor_of = 1.0
    for axis_at, shards_of in cuts:
        draws = jax.random.uniform(jax.random.fold_in(jax.random.fold_in(rng, 6), axis_at), (shards_of,), jnp.float32, low / len(cuts), high / len(cuts))
        factor_of = factor_of * jnp.repeat(jnp.exp(draws), shape[axis_at] // shards_of).reshape((-1,) + (1,) * (len(shape) - 1 - axis_at))
    return factor_of


def skewed_wide(stream_key, dims, amount, lean):
    loads = [min(1 << octave, amount + 1 - (1 << octave)) * (1 << 20) // math.isqrt((1 << octave) ** lean) + 1 for octave in range((amount + 1).bit_length()) if 1 << octave <= amount]
    width = 1 + sum(loads) // (1 << 30)
    table = np.cumsum(np.array([max(1, weight // width) for weight in loads]))
    pick = jax.random.randint(jax.random.fold_in(stream_key, 1), dims, 0, int(table[len(loads) - 1]))
    start = jnp.left_shift(1, jnp.searchsorted(jnp.asarray(table, jnp.int32), pick, side="right").astype(jnp.int32))
    grade = start - 1 + jax.random.randint(jax.random.fold_in(stream_key, 4), dims, 0, 1 << 30) % jnp.minimum(start, amount + 1 - start)
    return jax.random.permutation(jax.random.fold_in(stream_key, 2), amount)[grade].astype(jnp.int32)


def gaussian(own_key, shape, scale, limit, cuts=(), dtype=jnp.bfloat16):
    array = scale * jax.random.normal(own_key, shape, jnp.float32)
    if cuts:
        array = array * steps_of(own_key, shape, cuts, -0.22, 0.18)
    return jnp.clip(array, -limit, limit).astype(dtype)


def setup_inputs(seed: int = 0) -> dict:
    seeds = jax.random.split(jax.random.key(seed), 7)
    return {
        "teacher_hidden": draw_teacher_hidden(jax.random.fold_in(seeds[6], 71), 0),
        "teacher_head": gaussian(seeds[1], (TEACHER_DIM, VOCABULARY), TEACHER_DIM ** -0.5, 0.0625, ((1, 32),)),
        "student_hidden": draw_student_hidden(jax.random.fold_in(seeds[6], 71), 0),
        "student_head": gaussian(seeds[3], (STUDENT_DIM, VOCABULARY), STUDENT_DIM ** -0.5, 0.09375, ((1, 32),)),
        "labels": with_ends(skewed_wide(seeds[4], (TOKENS,), VOCABULARY, 2), jax.random.fold_in(seeds[4], 3), 0, VOCABULARY - 1).astype(jnp.int32),
        "owner_map": jax.random.permutation(seeds[5], TOKENS).astype(jnp.int32),
    }


def row_terms(teacher_rows, student_rows, teacher_lse, student_lse, weight, reverse, hits):
    log_teacher = teacher_rows - teacher_lse[:, None]
    log_student = student_rows - student_lse[:, None]
    teacher_prob = jnp.exp(log_teacher)
    student_prob = jnp.exp(log_student)
    mixed = weight[:, None] * (student_prob - teacher_prob)
    mixed = mixed + (1.0 - weight)[:, None] * student_prob * (log_student - log_teacher - reverse[:, None])
    mixed = mixed + student_prob - hits.astype(jnp.float32)
    return (mixed / TOKENS).astype(jnp.bfloat16)


def whole_rows(teacher_rows, student_rows, hits):
    teacher_top = jnp.max(teacher_rows, axis=1)
    student_top = jnp.max(student_rows, axis=1)
    teacher_lse = teacher_top + jnp.log(jnp.sum(jnp.exp(teacher_rows - teacher_top[:, None]), axis=1))
    student_lse = student_top + jnp.log(jnp.sum(jnp.exp(student_rows - student_top[:, None]), axis=1))
    log_teacher = teacher_rows - teacher_lse[:, None]
    log_student = student_rows - student_lse[:, None]
    teacher_prob = jnp.exp(log_teacher)
    student_prob = jnp.exp(log_student)
    entropy = -jnp.sum(teacher_prob * log_teacher, axis=1)
    weight = entropy / math.log(VOCABULARY)
    forward = jnp.sum(teacher_prob * (log_teacher - log_student), axis=1)
    reverse = jnp.sum(student_prob * (log_student - log_teacher), axis=1)
    cross = student_lse - jnp.sum(jnp.where(hits, student_rows, 0.0), axis=1)
    loss = weight * forward + (1.0 - weight) * reverse + cross
    return loss, row_terms(teacher_rows, student_rows, teacher_lse, student_lse, weight, reverse, hits)


def reference(teacher_hidden, teacher_head, student_hidden, student_head, labels, owner_map):
    ordered = jnp.take(teacher_hidden, owner_map, axis=0)
    teacher_logits = jnp.dot(ordered, teacher_head, preferred_element_type=jnp.float32)
    student_logits = jnp.dot(student_hidden, student_head, preferred_element_type=jnp.float32)
    hits = labels[:, None] == lax.iota(jnp.int32, VOCABULARY)[None, :]
    token_loss, grad_logits = whole_rows(teacher_logits, student_logits, hits)
    grad_head = jnp.dot(student_hidden.T, grad_logits, preferred_element_type=jnp.float32).astype(jnp.bfloat16)
    grad_hidden = jnp.dot(grad_logits, student_head.T, preferred_element_type=jnp.float32).astype(jnp.bfloat16)
    return (token_loss, grad_head, grad_hidden)
```

```python
import functools
import math

import jax
import jax.numpy as jnp
import numpy as np
from jax import lax
from jax.experimental import pallas as pl
from jax.experimental.pallas import tpu as pltpu
from jax.sharding import PartitionSpec as P

MESH = pl.DeviceIdType.MESH
FOLD = 4
SUB = 16
WIDE = 1024
CHUNK_S = 512
SLOTS = 3


def up(value, step):
    return -(-value // step) * step


def windows(rows):
    return [(q * rows // SUB * SUB, up((q + 1) * rows, SUB)) for q in range(FOLD)]


def tables(rows, groups, ring):
    half, line = groups // 2, ring // 2
    owners = [
        (x * 2 + c) * ring + z * 2 + y
        for c in range(2) for x in range(half) for y in range(2) for z in range(line)
    ]
    packed = []
    for q, (low, high) in enumerate(windows(rows)):
        for owner in owners:
            for o in range(low, high):
                r = o - q * rows
                packed.append(owner * rows + r if 0 <= r < rows else -1)
    padded = []
    for owner in owners:
        for o in range(up(rows, SUB)):
            padded.append(owner * rows + o if o < rows else -1)
    return np.array(packed, np.int32)[None, :], np.array(padded, np.int32)[:, None]


def fused(
    rows, groups, ring,
    th, sh, owner_col, label_col, token_row, token_col, t_head, s_head,
    loss_ref, g_out, h_out, gh_ref,
    buf_t, buf_s, heads, acc_t, acc_s, select, piece, hid, grads, place,
    st, stat_col, row_mat, col_mat, rs, rc, rxa, rxb, rya, ryb, rz,
    head_sem, out_sem, send_t, recv_t, send_s, recv_s, send_st, recv_st, send_r, recv_r,
):
    half, line = groups // 2, ring // 2
    devices = groups * ring
    mid = line // 2
    n_t, n_s = buf_t.shape[0], buf_s.shape[0]
    tokens, vocab = acc_t.shape
    grp, tp = lax.axis_index("grp"), lax.axis_index("tp")
    x, c = grp // 2, grp % 2
    z, y = tp // 2, tp % 2
    at_c = (x * 2 + 1 - c, tp)
    at_x = ((1 - x) * 2 + c, tp)
    at_y = (grp, z * 2 + 1 - y)
    at_z = [(grp, lax.rem(z + o, line) * 2 + y) for o in range(1, line)]

    def remote(src, dst, send, recv, device):
        return pltpu.make_async_remote_copy(
            src_ref=src, dst_ref=dst, send_sem=send, recv_sem=recv,
            device_id=device, device_id_type=MESH,
        )

    def load_head(h, slot):
        wide = heads.shape[1]
        narrow = hid.shape[2]

        def t_copy():
            return pltpu.make_async_copy(
                t_head.at[pl.ds(pl.multiple_of(h * wide, wide), wide)], heads.at[slot], head_sem.at[slot])

        def s_copy():
            k = lax.rem(h - n_t, n_s)
            return pltpu.make_async_copy(
                s_head.at[pl.ds(pl.multiple_of(k * narrow, narrow), narrow)],
                heads.at[slot, pl.ds(0, narrow)], head_sem.at[slot])

        return t_copy, s_copy

    def start_head(h):
        slot = lax.rem(h, SLOTS)
        t_copy, s_copy = load_head(h, slot)

        @pl.when(h < n_t)
        def _():
            t_copy().start()

        @pl.when(jnp.logical_and(h >= n_t, h < n_t + 2 * n_s))
        def _():
            s_copy().start()

    start_head(jnp.int32(0))
    start_head(jnp.int32(1))

    barrier = pltpu.get_barrier_semaphore()
    for device in (at_c, at_x, at_y, *at_z):
        pl.semaphore_signal(barrier, inc=1, device_id=device, device_id_type=MESH)
    pl.semaphore_wait(barrier, line + 2)

    def stage(buf, i, send, recv, number):
        b = buf.at[i]
        if number == 0:
            return [
                remote(b.at[c, x, y, z], b.at[c, x, y, z], send.at[i, o], recv.at[i, o], at_z[o])
                for o in range(line - 1)
            ]
        k = line - 1
        first, last = pl.ds(0, mid), pl.ds(mid, line - mid)
        if number == 1:
            one, two = b.at[c, x, y, first], b.at[c, x, y, last]
            return [
                remote(one, one, send.at[i, k], recv.at[i, k], at_y),
                remote(two, two, send.at[i, k + 1], recv.at[i, k + 1], at_x),
            ]
        if number == 2:
            one, two = b.at[c, x, :, first], b.at[c, :, y, last]
            return [
                remote(one, one, send.at[i, k + 2], recv.at[i, k + 2], at_x),
                remote(two, two, send.at[i, k + 3], recv.at[i, k + 3], at_y),
            ]
        return [remote(b.at[c], b.at[c], send.at[i, k + 4], recv.at[i, k + 4], at_c)]

    def advance(buf, i, send, recv, number):
        if number > 0:
            for copy in stage(buf, i, send, recv, number - 1):
                copy.wait_recv()
        if number < 4:
            for copy in stage(buf, i, send, recv, number):
                copy.start()

    def forward(step):
        for number in (0, 3, 2, 1):
            g = step - number

            @pl.when(jnp.logical_and(g >= 0, g < n_t))
            def _():
                advance(buf_t, g, send_t, recv_t, number)

            @pl.when(jnp.logical_and(g >= n_t, g < n_t + n_s))
            def _():
                advance(buf_s, g - n_t, send_s, recv_s, number)

    for i in range(n_t):
        buf_t[i, c, x, y, z] = th[i]
    for i in range(n_s):
        buf_s[i, c, x, y, z] = sh[i]

    spans = windows(rows)

    def set_select(column):
        at = 0
        for low, high in spans:
            size = devices * (high - low)

            @pl.loop(0, tokens // 32)
            def _(r):
                these = pl.ds(pl.multiple_of(r * 32, 32), 32)
                ids = lax.broadcasted_iota(jnp.int32, (32, 1), 0) + r * 32 if column is None else column[these, :]
                hit = ids == token_row[:, at:at + size]
                select[these, at:at + size] = jnp.where(hit, 1.0, 0.0).astype(jnp.bfloat16)

            at += size

    def unfold(buf, i, q):
        low, high = spans[q]
        at = devices * sum(h - l for l, h in spans[:q])
        size = devices * (high - low)
        block = buf[i, :, :, :, :, low:high, :].reshape(size, buf.shape[-1])
        return jnp.dot(select[:, at:at + size], block, preferred_element_type=jnp.float32).astype(jnp.bfloat16)

    tile = 512 if vocab % 512 == 0 else 256

    forward(jnp.int32(0))
    acc_t[...] = jnp.zeros_like(acc_t)
    set_select(owner_col)
    forward(jnp.int32(1))
    acc_s[...] = jnp.zeros_like(acc_s)
    place[...] = jnp.where(
        token_col[...] == lax.broadcasted_iota(jnp.int32, place.shape, 1), 1.0, 0.0
    ).astype(jnp.bfloat16)
    forward(jnp.int32(2))
    forward(jnp.int32(3))

    @pl.loop(0, n_t)
    def _(i):
        forward(i + 4)
        start_head(i + 2)
        advance(buf_t, i, send_t, recv_t, 4)
        width = buf_t.shape[-1]
        for q in range(FOLD):
            piece[:, q * width:(q + 1) * width] = unfold(buf_t, i, q)
        slot = lax.rem(i, SLOTS)
        load_head(i, slot)[0]().wait()

        @pl.loop(0, vocab // tile)
        def _(n):
            cols = pl.ds(pl.multiple_of(n * tile, tile), tile)
            acc_t[:, cols] += jnp.dot(piece[...], heads[slot, :, cols], preferred_element_type=jnp.float32)

    student = hid.shape[2]
    set_select(None)

    @pl.loop(0, n_s)
    def _(i):
        h = i + n_t
        forward(h + 4)
        start_head(h + 2)
        advance(buf_s, i, send_s, recv_s, 4)
        width = buf_s.shape[-1]
        for q in range(FOLD):
            hid[i, :, q * width:(q + 1) * width] = unfold(buf_s, i, q)
        slot = lax.rem(h, SLOTS)
        load_head(h, slot)[1]().wait()

        @pl.loop(0, vocab // tile)
        def _(n):
            cols = pl.ds(pl.multiple_of(n * tile, tile), tile)
            acc_s[:, cols] += jnp.dot(
                hid[i], heads[slot, pl.ds(0, student), cols], preferred_element_type=jnp.float32)

    hid_copy = pltpu.make_async_copy(hid, h_out, out_sem.at[0])
    hid_copy.start()

    base = (grp * ring + tp) * vocab

    @pl.loop(0, tokens // 8)
    def _(r):
        these = pl.ds(pl.multiple_of(r * 8, 8), 8)
        t, s = acc_t[these, :], acc_s[these, :]
        t_top = jnp.max(t, axis=1, keepdims=True)
        s_top = jnp.max(s, axis=1, keepdims=True)
        t_exp, s_exp = jnp.exp(t - t_top), jnp.exp(s - s_top)
        differ = t - s
        hits = label_col[these, :] == lax.broadcasted_iota(jnp.int32, t.shape, 1) + base
        values = [
            t_top, s_top,
            jnp.sum(t_exp, axis=1, keepdims=True),
            jnp.sum(s_exp, axis=1, keepdims=True),
            jnp.sum(t_exp * t, axis=1, keepdims=True),
            jnp.sum(t_exp * differ, axis=1, keepdims=True),
            jnp.sum(s_exp * differ, axis=1, keepdims=True),
            jnp.sum(jnp.where(hits, s, 0.0), axis=1, keepdims=True),
        ]
        lane = lax.broadcasted_iota(jnp.int32, (8, 128), 1)
        out = jnp.zeros((8, 128), jnp.float32)
        for k, value in enumerate(values):
            out = jnp.where(lane == k, value, out)
        stat_col[these, :] = out

    st[0, c, x, y, z] = jnp.transpose(stat_col[...])[0:8, :]
    for number in range(5):
        advance(st, 0, send_st, recv_st, number)

    cells = [(cc, xx, yy) for cc in range(2) for xx in range(half) for yy in range(2)]

    def highest(k, best):
        for cc, xx, yy in cells:
            best = jnp.maximum(best, st[0, cc, xx, yy, k])
        return best

    top = lax.fori_loop(0, line, highest, jnp.full((8, tokens), -jnp.inf, jnp.float32))
    row = lax.broadcasted_iota(jnp.int32, (8, tokens), 0)
    of_student = jnp.logical_or(row == 3, row == 6)

    def gathered(k, sums):
        for cc, xx, yy in cells:
            one = st[0, cc, xx, yy, k]
            shift = jnp.exp(one - top)
            scale = jnp.where(of_student, shift[1:2, :], jnp.where(row == 7, 1.0, shift[0:1, :]))
            sums = sums + one * scale
        return sums

    sums = lax.fori_loop(0, line, gathered, jnp.zeros((8, tokens), jnp.float32))
    t_total, s_total, t_moment, forward_moment, reverse_moment, label_logit = (
        sums[k:k + 1, :] for k in range(2, 8))
    t_lse = top[0:1] + jnp.log(t_total)
    s_lse = top[1:2] + jnp.log(s_total)
    weight = (t_lse - t_moment / t_total) / math.log(vocab * devices)
    ahead = forward_moment / t_total - t_lse + s_lse
    back = -reverse_moment / s_total - s_lse + t_lse
    loss_ref[...] = weight * ahead + (1.0 - weight) * back + s_lse - label_logit

    row_mat[...] = jnp.zeros_like(row_mat)
    for k, value in enumerate((t_lse, s_lse, weight, back)):
        row_mat[k:k + 1, :] = value
    col_mat[...] = jnp.transpose(row_mat[...])

    @pl.loop(0, tokens // SUB)
    def _(r):
        these = pl.ds(pl.multiple_of(r * SUB, SUB), SUB)
        cols = col_mat[these, :]
        log_t = acc_t[these, :] - cols[:, 0:1]
        log_s = acc_s[these, :] - cols[:, 1:2]
        w, rev = cols[:, 2:3], cols[:, 3:4]
        t_prob, s_prob = jnp.exp(log_t), jnp.exp(log_s)
        hits = label_col[these, :] == lax.broadcasted_iota(jnp.int32, log_t.shape, 1) + base
        mixed = w * (s_prob - t_prob) + (1.0 - w) * s_prob * (log_s - log_t - rev)
        mixed = mixed + s_prob - jnp.where(hits, 1.0, 0.0)
        grads[these, :] = (mixed / tokens).astype(jnp.bfloat16)

    grad_copy = pltpu.make_async_copy(grads, g_out, out_sem.at[1])
    grad_copy.start()

    def back_stage(j, number):
        b = rs.at[j]
        first, last = pl.ds(0, mid), pl.ds(mid, line - mid)
        if number == 0:
            return [remote(b.at[1 - c], rc.at[j], send_r.at[j, 0], recv_r.at[j, 0], at_c)]
        if number == 1:
            return [
                remote(b.at[c, 1 - x, :, first], rxa.at[j], send_r.at[j, 1], recv_r.at[j, 1], at_x),
                remote(b.at[c, :, 1 - y, last], ryb.at[j], send_r.at[j, 2], recv_r.at[j, 2], at_y),
            ]
        if number == 2:
            return [
                remote(b.at[c, x, 1 - y, first], rya.at[j], send_r.at[j, 3], recv_r.at[j, 3], at_y),
                remote(b.at[c, 1 - x, y, last], rxb.at[j], send_r.at[j, 4], recv_r.at[j, 4], at_x),
            ]
        return [
            remote(b.at[c, x, y, lax.rem(z + o + 1, line)], rz.at[j, o],
                   send_r.at[j, 5 + o], recv_r.at[j, 5 + o], at_z[o])
            for o in range(line - 1)
        ]

    def plus(one, two):
        return (one.astype(jnp.float32) + two.astype(jnp.float32)).astype(jnp.bfloat16)

    def back_advance(j, number):
        if number > 0:
            for copy in back_stage(j, number - 1):
                copy.wait_recv()
        if number == 1:
            for k in range(half):
                rs[j, c, k] = plus(rs[j, c, k], rc[j, k])
        elif number == 2:
            rs[j, c, x, :, 0:mid] = plus(rs[j, c, x, :, 0:mid], rxa[j])
            rs[j, c, :, y, mid:] = plus(rs[j, c, :, y, mid:], ryb[j])
        elif number == 3:
            rs[j, c, x, y, 0:mid] = plus(rs[j, c, x, y, 0:mid], rya[j])
            rs[j, c, x, y, mid:] = plus(rs[j, c, x, y, mid:], rxb[j])
        elif number == 4:
            own = rs[j, c, x, y, z].astype(jnp.float32)
            for o in range(line - 1):
                own = own + rz[j, o].astype(jnp.float32)
            gh_ref[j] = own.astype(jnp.bfloat16)
        if number < 4:
            for copy in back_stage(j, number):
                copy.start()

    def back_forward(step):
        for number in (4, 3, 2, 1):
            j = step - number

            @pl.when(jnp.logical_and(j >= 0, j < n_s))
            def _():
                back_advance(j, number)

    pad = up(rows, SUB)

    @pl.loop(0, n_s)
    def _(j):
        h = j + n_t + n_s
        start_head(h + 2)
        slot = lax.rem(h, SLOTS)
        load_head(h, slot)[1]().wait()
        part = lax.dot_general(
            grads[...], heads[slot, pl.ds(0, student), :], (((1,), (1,)), ((), ())),
            preferred_element_type=jnp.float32).astype(jnp.bfloat16)
        size = 2 * line * pad
        for cc in range(2):
            for xx in range(half):
                at = (cc * half + xx) * size
                block = jnp.dot(place[at:at + size, :], part, preferred_element_type=jnp.float32)
                rs[j, cc, xx] = block.astype(jnp.bfloat16).reshape(2, line, pad, student)
        back_advance(j, 0)
        back_forward(j)

    for step in range(4):
        back_forward(jnp.int32(n_s + step))

    @pl.loop(0, n_t)
    def _(i):
        for number in range(4):
            for copy in stage(buf_t, i, send_t, recv_t, number):
                copy.wait_send()

    @pl.loop(0, n_s)
    def _(i):
        for number in range(4):
            for copy in stage(buf_s, i, send_s, recv_s, number):
                copy.wait_send()
            for copy in back_stage(i, number):
                copy.wait_send()

    for number in range(4):
        for copy in stage(st, 0, send_st, recv_st, number):
            copy.wait_send()
    hid_copy.wait()
    grad_copy.wait()


def head_kernel(hid, grads, out):
    out[...] = lax.dot_general(
        hid[0], grads[...], (((0,), (0,)), ((), ())), preferred_element_type=jnp.float32
    ).astype(jnp.bfloat16)


def fold(hidden, chunk, block):
    rows, dim = hidden.shape
    parts = dim // chunk
    folded = hidden.reshape(rows, parts, FOLD, chunk // FOLD).transpose(1, 2, 0, 3)
    folded = folded.reshape(parts, FOLD * rows, chunk // FOLD)
    return jnp.pad(folded, ((0, 0), (0, block - FOLD * rows), (0, 0)))


def shards(groups, ring, teacher_hidden, teacher_head, student_hidden, student_head, labels, owner_map):
    rows, t_dim = teacher_hidden.shape
    s_dim, vocab = student_head.shape
    tokens = labels.shape[0]
    half, line, devices = groups // 2, ring // 2, groups * ring
    mid = line // 2
    block, pad = up(FOLD * rows, SUB), up(rows, SUB)
    chunk_t = WIDE if vocab > WIDE else CHUNK_S
    n_t, n_s = t_dim // chunk_t, s_dim // CHUNK_S
    packed, padded = tables(rows, groups, ring)
    vmem = pl.BlockSpec(memory_space=pltpu.VMEM)
    anywhere = pl.BlockSpec(memory_space=pl.ANY)
    bf, f32 = jnp.bfloat16, jnp.float32
    dma = pltpu.SemaphoreType.DMA
    cube = (2, half, 2, line)
    loss, grads, hid, mine = pl.pallas_call(
        functools.partial(fused, rows, groups, ring),
        out_shape=(
            jax.ShapeDtypeStruct((1, tokens), f32),
            jax.ShapeDtypeStruct((tokens, vocab), bf),
            jax.ShapeDtypeStruct((n_s, tokens, CHUNK_S), bf),
            jax.ShapeDtypeStruct((n_s, pad, CHUNK_S), bf),
        ),
        in_specs=[vmem] * 6 + [anywhere] * 2,
        out_specs=(vmem, anywhere, anywhere, vmem),
        scratch_shapes=[
            pltpu.VMEM((n_t, *cube, block, chunk_t // FOLD), bf),
            pltpu.VMEM((n_s, *cube, block, CHUNK_S // FOLD), bf),
            pltpu.VMEM((SLOTS, chunk_t, vocab), bf),
            pltpu.VMEM((tokens, vocab), f32),
            pltpu.VMEM((tokens, vocab), f32),
            pltpu.VMEM((tokens, packed.shape[1]), bf),
            pltpu.VMEM((tokens, chunk_t), bf),
            pltpu.VMEM((n_s, tokens, CHUNK_S), bf),
            pltpu.VMEM((tokens, vocab), bf),
            pltpu.VMEM((devices * pad, tokens), bf),
            pltpu.VMEM((1, *cube, 8, tokens), f32),
            pltpu.VMEM((tokens, 128), f32),
            pltpu.VMEM((128, tokens), f32),
            pltpu.VMEM((tokens, 128), f32),
            pltpu.VMEM((n_s, *cube, pad, CHUNK_S), bf),
            pltpu.VMEM((n_s, half, 2, line, pad, CHUNK_S), bf),
            pltpu.VMEM((n_s, 2, mid, pad, CHUNK_S), bf),
            pltpu.VMEM((n_s, line - mid, pad, CHUNK_S), bf),
            pltpu.VMEM((n_s, mid, pad, CHUNK_S), bf),
            pltpu.VMEM((n_s, half, line - mid, pad, CHUNK_S), bf),
            pltpu.VMEM((n_s, line - 1, pad, CHUNK_S), bf),
            dma((SLOTS,)), dma((2,)),
            dma((n_t, line + 4)), dma((n_t, line + 4)),
            dma((n_s, line + 4)), dma((n_s, line + 4)),
            dma((1, line + 4)), dma((1, line + 4)),
            dma((n_s, line + 4)), dma((n_s, line + 4)),
        ],
        compiler_params=pltpu.CompilerParams(
            collective_id=0, has_side_effects=True, vmem_limit_bytes=62 * 2**20),
        cost_estimate=pl.CostEstimate(
            flops=2 * tokens * vocab * (t_dim + 2 * s_dim),
            bytes_accessed=2 * vocab * (t_dim + 2 * s_dim), transcendentals=4 * tokens * vocab),
    )(
        fold(teacher_hidden, chunk_t, block), fold(student_hidden, CHUNK_S, block),
        owner_map[:, None], labels[:, None], jnp.asarray(packed), jnp.asarray(padded),
        teacher_head, student_head,
    )
    grad_head = pl.pallas_call(
        head_kernel,
        out_shape=jax.ShapeDtypeStruct((s_dim, vocab), bf),
        grid=(n_s,),
        in_specs=[
            pl.BlockSpec((1, tokens, CHUNK_S), lambda i: (i, 0, 0)),
            pl.BlockSpec((tokens, vocab), lambda i: (0, 0)),
        ],
        out_specs=pl.BlockSpec((CHUNK_S, vocab), lambda i: (i, 0)),
        compiler_params=pltpu.CompilerParams(vmem_limit_bytes=40 * 2**20),
        cost_estimate=pl.CostEstimate(
            flops=2 * tokens * vocab * s_dim, bytes_accessed=2 * vocab * s_dim, transcendentals=0),
    )(hid, grads)
    position = lax.axis_index("grp") * ring + lax.axis_index("tp")
    token_loss = lax.dynamic_slice_in_dim(loss[0], position * rows, rows)
    grad_hidden = mine[:, :rows, :].transpose(1, 0, 2).reshape(rows, s_dim)
    return token_loss, grad_head, grad_hidden


def solution(mesh):
    groups, ring = mesh.shape["grp"], mesh.shape["tp"]
    in_specs = (
        P(("grp", "tp"), None),
        P(None, ("grp", "tp")),
        P(("grp", "tp"), None),
        P(None, ("grp", "tp")),
        P(),
        P(),
    )
    out_specs = (P(("grp", "tp")), P(None, ("grp", "tp")), P(("grp", "tp"), None))
    return jax.shard_map(
        functools.partial(shards, groups, ring),
        mesh=mesh, in_specs=in_specs, out_specs=out_specs, check_vma=False)
```

```python
import functools
import math

import jax
import jax.numpy as jnp
import numpy as np
from jax import lax
from jax.experimental import pallas as pl
from jax.experimental.pallas import tpu as pltpu
from jax.sharding import PartitionSpec as P

MESH = pl.DeviceIdType.MESH
FOLD = 4
SUB = 16
WIDE = 1024
CHUNK_S = 512
SLOTS = 3


def up(value, step):
    return -(-value // step) * step


def windows(rows):
    return [(q * rows // SUB * SUB, up((q + 1) * rows, SUB)) for q in range(FOLD)]


def tables(rows, groups, ring):
    half, line = groups // 2, ring // 2
    owners = [
        (x * 2 + c) * ring + z * 2 + y
        for c in range(2) for x in range(half) for y in range(2) for z in range(line)
    ]
    packed = []
    for q, (low, high) in enumerate(windows(rows)):
        for owner in owners:
            for o in range(low, high):
                r = o - q * rows
                packed.append(owner * rows + r if 0 <= r < rows else -1)
    padded = []
    for owner in owners:
        for o in range(up(rows, SUB)):
            padded.append(owner * rows + o if o < rows else -1)
    return np.array(packed, np.int32)[None, :], np.array(padded, np.int32)[:, None]


def fused(
    rows, groups, ring,
    th, sh, owner_col, label_col, token_row, token_col, t_head, s_head,
    loss_ref, g_out, h_out, gh_ref,
    buf_t, buf_s, heads, acc_t, acc_s, select, piece, hid, grads, place,
    st, stat_col, row_mat, col_mat, rs, rc, rxa, rxb, rya, ryb, rz,
    head_sem, out_sem, send_t, recv_t, send_s, recv_s, send_st, recv_st, send_r, recv_r,
):
    half, line = groups // 2, ring // 2
    devices = groups * ring
    mid = line // 2
    n_t, n_s = buf_t.shape[0], buf_s.shape[0]
    tokens, vocab = acc_t.shape
    grp, tp = lax.axis_index("grp"), lax.axis_index("tp")
    x, c = grp // 2, grp % 2
    z, y = tp // 2, tp % 2
    at_c = (x * 2 + 1 - c, tp)
    at_x = ((1 - x) * 2 + c, tp)
    at_y = (grp, z * 2 + 1 - y)
    at_z = [(grp, lax.rem(z + o, line) * 2 + y) for o in range(1, line)]

    def remote(src, dst, send, recv, device):
        return pltpu.make_async_remote_copy(
            src_ref=src, dst_ref=dst, send_sem=send, recv_sem=recv,
            device_id=device, device_id_type=MESH,
        )

    def load_head(h, slot):
        wide = heads.shape[1]
        narrow = hid.shape[2]

        def t_copy():
            return pltpu.make_async_copy(
                t_head.at[pl.ds(pl.multiple_of(h * wide, wide), wide)], heads.at[slot], head_sem.at[slot])

        def s_copy():
            k = lax.rem(h - n_t, n_s)
            return pltpu.make_async_copy(
                s_head.at[pl.ds(pl.multiple_of(k * narrow, narrow), narrow)],
                heads.at[slot, pl.ds(0, narrow)], head_sem.at[slot])

        return t_copy, s_copy

    def start_head(h):
        slot = lax.rem(h, SLOTS)
        t_copy, s_copy = load_head(h, slot)

        @pl.when(h < n_t)
        def _():
            t_copy().start()

        @pl.when(jnp.logical_and(h >= n_t, h < n_t + 2 * n_s))
        def _():
            s_copy().start()

    start_head(jnp.int32(0))
    start_head(jnp.int32(1))

    barrier = pltpu.get_barrier_semaphore()
    for device in (at_c, at_x, at_y, *at_z):
        pl.semaphore_signal(barrier, inc=1, device_id=device, device_id_type=MESH)
    pl.semaphore_wait(barrier, line + 2)

    def stage(buf, i, send, recv, number):
        b = buf.at[i]
        if number == 0:
            return [
                remote(b.at[c, x, y, z], b.at[c, x, y, z], send.at[i, o], recv.at[i, o], at_z[o])
                for o in range(line - 1)
            ]
        k = line - 1
        first, last = pl.ds(0, mid), pl.ds(mid, line - mid)
        if number == 1:
            one, two = b.at[c, x, y, first], b.at[c, x, y, last]
            return [
                remote(one, one, send.at[i, k], recv.at[i, k], at_y),
                remote(two, two, send.at[i, k + 1], recv.at[i, k + 1], at_x),
            ]
        if number == 2:
            one, two = b.at[c, x, :, first], b.at[c, :, y, last]
            return [
                remote(one, one, send.at[i, k + 2], recv.at[i, k + 2], at_x),
                remote(two, two, send.at[i, k + 3], recv.at[i, k + 3], at_y),
            ]
        return [remote(b.at[c], b.at[c], send.at[i, k + 4], recv.at[i, k + 4], at_c)]

    def advance(buf, i, send, recv, number):
        if number > 0:
            for copy in stage(buf, i, send, recv, number - 1):
                copy.wait_recv()
        if number < 4:
            for copy in stage(buf, i, send, recv, number):
                copy.start()

    def forward(step):
        for number in (0, 3, 2, 1):
            g = step - number

            @pl.when(jnp.logical_and(g >= 0, g < n_t))
            def _():
                advance(buf_t, g, send_t, recv_t, number)

            @pl.when(jnp.logical_and(g >= n_t, g < n_t + n_s))
            def _():
                advance(buf_s, g - n_t, send_s, recv_s, number)

    for i in range(n_t):
        buf_t[i, c, x, y, z] = th[i]
    for i in range(n_s):
        buf_s[i, c, x, y, z] = sh[i]

    spans = windows(rows)

    def set_select(column):
        at = 0
        for low, high in spans:
            size = devices * (high - low)

            @pl.loop(0, tokens // 32)
            def _(r):
                these = pl.ds(pl.multiple_of(r * 32, 32), 32)
                ids = lax.broadcasted_iota(jnp.int32, (32, 1), 0) + r * 32 if column is None else column[these, :]
                hit = ids == token_row[:, at:at + size]
                select[these, at:at + size] = jnp.where(hit, 1.0, 0.0).astype(jnp.bfloat16)

            at += size

    def unfold(buf, i, q):
        low, high = spans[q]
        at = devices * sum(h - l for l, h in spans[:q])
        size = devices * (high - low)
        block = buf[i, :, :, :, :, low:high, :].reshape(size, buf.shape[-1])
        return jnp.dot(select[:, at:at + size], block, preferred_element_type=jnp.float32).astype(jnp.bfloat16)

    tile = 1024 if vocab % 1024 == 0 else 256

    forward(jnp.int32(0))
    acc_t[...] = jnp.zeros_like(acc_t)
    set_select(owner_col)
    forward(jnp.int32(1))
    acc_s[...] = jnp.zeros_like(acc_s)
    place[...] = jnp.where(
        token_col[...] == lax.broadcasted_iota(jnp.int32, place.shape, 1), 1.0, 0.0
    ).astype(jnp.bfloat16)
    forward(jnp.int32(2))
    forward(jnp.int32(3))

    @pl.loop(0, n_t)
    def _(i):
        forward(i + 4)
        start_head(i + 2)
        advance(buf_t, i, send_t, recv_t, 4)
        width = buf_t.shape[-1]
        for q in range(FOLD):
            piece[:, q * width:(q + 1) * width] = unfold(buf_t, i, q)
        slot = lax.rem(i, SLOTS)
        load_head(i, slot)[0]().wait()

        @pl.loop(0, vocab // tile)
        def _(n):
            cols = pl.ds(pl.multiple_of(n * tile, tile), tile)
            acc_t[:, cols] += jnp.dot(piece[...], heads[slot, :, cols], preferred_element_type=jnp.float32)

    student = hid.shape[2]
    set_select(None)

    @pl.loop(0, n_s)
    def _(i):
        h = i + n_t
        forward(h + 4)
        start_head(h + 2)
        advance(buf_s, i, send_s, recv_s, 4)
        width = buf_s.shape[-1]
        for q in range(FOLD):
            hid[i, :, q * width:(q + 1) * width] = unfold(buf_s, i, q)
        slot = lax.rem(h, SLOTS)
        load_head(h, slot)[1]().wait()

        @pl.loop(0, vocab // tile)
        def _(n):
            cols = pl.ds(pl.multiple_of(n * tile, tile), tile)
            acc_s[:, cols] += jnp.dot(
                hid[i], heads[slot, pl.ds(0, student), cols], preferred_element_type=jnp.float32)

    hid_copy = pltpu.make_async_copy(hid, h_out, out_sem.at[0])
    hid_copy.start()

    base = (grp * ring + tp) * vocab

    @pl.loop(0, tokens // 8, unroll=4)
    def _(r):
        these = pl.ds(pl.multiple_of(r * 8, 8), 8)
        t, s = acc_t[these, :], acc_s[these, :]
        t_top = jnp.max(t, axis=1, keepdims=True)
        s_top = jnp.max(s, axis=1, keepdims=True)
        t_exp, s_exp = jnp.exp(t - t_top), jnp.exp(s - s_top)
        differ = t - s
        hits = label_col[these, :] == lax.broadcasted_iota(jnp.int32, t.shape, 1) + base
        values = [
            t_top, s_top,
            jnp.sum(t_exp, axis=1, keepdims=True),
            jnp.sum(s_exp, axis=1, keepdims=True),
            jnp.sum(t_exp * t, axis=1, keepdims=True),
            jnp.sum(t_exp * differ, axis=1, keepdims=True),
            jnp.sum(s_exp * differ, axis=1, keepdims=True),
            jnp.sum(jnp.where(hits, s, 0.0), axis=1, keepdims=True),
        ]
        lane = lax.broadcasted_iota(jnp.int32, (8, 128), 1)
        out = jnp.zeros((8, 128), jnp.float32)
        for k, value in enumerate(values):
            out = jnp.where(lane == k, value, out)
        stat_col[these, :] = out

    st[0, c, x, y, z] = jnp.transpose(stat_col[...])[0:8, :]
    for number in range(5):
        advance(st, 0, send_st, recv_st, number)

    cells = [(cc, xx, yy) for cc in range(2) for xx in range(half) for yy in range(2)]

    def highest(k, best):
        for cc, xx, yy in cells:
            best = jnp.maximum(best, st[0, cc, xx, yy, k])
        return best

    top = lax.fori_loop(0, line, highest, jnp.full((8, tokens), -jnp.inf, jnp.float32))
    row = lax.broadcasted_iota(jnp.int32, (8, tokens), 0)
    of_student = jnp.logical_or(row == 3, row == 6)

    def gathered(k, sums):
        for cc, xx, yy in cells:
            one = st[0, cc, xx, yy, k]
            shift = jnp.exp(one - top)
            scale = jnp.where(of_student, shift[1:2, :], jnp.where(row == 7, 1.0, shift[0:1, :]))
            sums = sums + one * scale
        return sums

    sums = lax.fori_loop(0, line, gathered, jnp.zeros((8, tokens), jnp.float32))
    t_total, s_total, t_moment, forward_moment, reverse_moment, label_logit = (
        sums[k:k + 1, :] for k in range(2, 8))
    t_lse = top[0:1] + jnp.log(t_total)
    s_lse = top[1:2] + jnp.log(s_total)
    weight = (t_lse - t_moment / t_total) / math.log(vocab * devices)
    ahead = forward_moment / t_total - t_lse + s_lse
    back = -reverse_moment / s_total - s_lse + t_lse
    loss_ref[...] = weight * ahead + (1.0 - weight) * back + s_lse - label_logit

    row_mat[...] = jnp.zeros_like(row_mat)
    for k, value in enumerate((t_lse, s_lse, weight, back)):
        row_mat[k:k + 1, :] = value
    col_mat[...] = jnp.transpose(row_mat[...])

    @pl.loop(0, tokens // SUB, unroll=2)
    def _(r):
        these = pl.ds(pl.multiple_of(r * SUB, SUB), SUB)
        cols = col_mat[these, :]
        log_t = acc_t[these, :] - cols[:, 0:1]
        log_s = acc_s[these, :] - cols[:, 1:2]
        w, rev = cols[:, 2:3], cols[:, 3:4]
        t_prob, s_prob = jnp.exp(log_t), jnp.exp(log_s)
        hits = label_col[these, :] == lax.broadcasted_iota(jnp.int32, log_t.shape, 1) + base
        mixed = w * (s_prob - t_prob) + (1.0 - w) * s_prob * (log_s - log_t - rev)
        mixed = mixed + s_prob - jnp.where(hits, 1.0, 0.0)
        grads[these, :] = (mixed * (1.0 / tokens)).astype(jnp.bfloat16)

    grad_copy = pltpu.make_async_copy(grads, g_out, out_sem.at[1])
    grad_copy.start()

    def back_stage(j, number):
        b = rs.at[j]
        first, last = pl.ds(0, mid), pl.ds(mid, line - mid)
        if number == 0:
            return [remote(b.at[1 - c], rc.at[j], send_r.at[j, 0], recv_r.at[j, 0], at_c)]
        if number == 1:
            return [
                remote(b.at[c, 1 - x, :, first], rxa.at[j], send_r.at[j, 1], recv_r.at[j, 1], at_x),
                remote(b.at[c, :, 1 - y, last], ryb.at[j], send_r.at[j, 2], recv_r.at[j, 2], at_y),
            ]
        if number == 2:
            return [
                remote(b.at[c, x, 1 - y, first], rya.at[j], send_r.at[j, 3], recv_r.at[j, 3], at_y),
                remote(b.at[c, 1 - x, y, last], rxb.at[j], send_r.at[j, 4], recv_r.at[j, 4], at_x),
            ]
        return [
            remote(b.at[c, x, y, lax.rem(z + o + 1, line)], rz.at[j, o],
                   send_r.at[j, 5 + o], recv_r.at[j, 5 + o], at_z[o])
            for o in range(line - 1)
        ]

    def plus(one, two):
        return (one.astype(jnp.float32) + two.astype(jnp.float32)).astype(jnp.bfloat16)

    def back_advance(j, number):
        if number > 0:
            for copy in back_stage(j, number - 1):
                copy.wait_recv()
        if number == 1:
            for k in range(half):
                rs[j, c, k] = plus(rs[j, c, k], rc[j, k])
        elif number == 2:
            rs[j, c, x, :, 0:mid] = plus(rs[j, c, x, :, 0:mid], rxa[j])
            rs[j, c, :, y, mid:] = plus(rs[j, c, :, y, mid:], ryb[j])
        elif number == 3:
            rs[j, c, x, y, 0:mid] = plus(rs[j, c, x, y, 0:mid], rya[j])
            rs[j, c, x, y, mid:] = plus(rs[j, c, x, y, mid:], rxb[j])
        elif number == 4:
            own = rs[j, c, x, y, z].astype(jnp.float32)
            for o in range(line - 1):
                own = own + rz[j, o].astype(jnp.float32)
            gh_ref[j] = own.astype(jnp.bfloat16)
        if number < 4:
            for copy in back_stage(j, number):
                copy.start()

    def back_forward(step):
        for number in (4, 3, 2, 1):
            j = step - number

            @pl.when(jnp.logical_and(j >= 0, j < n_s))
            def _():
                back_advance(j, number)

    pad = up(rows, SUB)

    @pl.loop(0, n_s)
    def _(j):
        h = j + n_t + n_s
        start_head(h + 2)
        slot = lax.rem(h, SLOTS)
        load_head(h, slot)[1]().wait()
        part = lax.dot_general(
            grads[...], heads[slot, pl.ds(0, student), :], (((1,), (1,)), ((), ())),
            preferred_element_type=jnp.float32).astype(jnp.bfloat16)
        size = 2 * line * pad
        for cc in range(2):
            for xx in range(half):
                at = (cc * half + xx) * size
                block = jnp.dot(place[at:at + size, :], part, preferred_element_type=jnp.float32)
                rs[j, cc, xx] = block.astype(jnp.bfloat16).reshape(2, line, pad, student)
        back_advance(j, 0)
        back_forward(j)

    for step in range(4):
        back_forward(jnp.int32(n_s + step))

    @pl.loop(0, n_t)
    def _(i):
        for number in range(4):
            for copy in stage(buf_t, i, send_t, recv_t, number):
                copy.wait_send()

    @pl.loop(0, n_s)
    def _(i):
        for number in range(4):
            for copy in stage(buf_s, i, send_s, recv_s, number):
                copy.wait_send()
            for copy in back_stage(i, number):
                copy.wait_send()

    for number in range(4):
        for copy in stage(st, 0, send_st, recv_st, number):
            copy.wait_send()
    hid_copy.wait()
    grad_copy.wait()


def head_kernel(hid, grads, out):
    out[...] = lax.dot_general(
        hid[0], grads[...], (((0,), (0,)), ((), ())), preferred_element_type=jnp.float32
    ).astype(jnp.bfloat16)


def fold(hidden, chunk, block):
    rows, dim = hidden.shape
    parts = dim // chunk
    folded = hidden.reshape(rows, parts, FOLD, chunk // FOLD).transpose(1, 2, 0, 3)
    folded = folded.reshape(parts, FOLD * rows, chunk // FOLD)
    return jnp.pad(folded, ((0, 0), (0, block - FOLD * rows), (0, 0)))


def shards(groups, ring, teacher_hidden, teacher_head, student_hidden, student_head, labels, owner_map):
    rows, t_dim = teacher_hidden.shape
    s_dim, vocab = student_head.shape
    tokens = labels.shape[0]
    half, line, devices = groups // 2, ring // 2, groups * ring
    mid = line // 2
    block, pad = up(FOLD * rows, SUB), up(rows, SUB)
    chunk_t = WIDE if vocab > WIDE else CHUNK_S
    n_t, n_s = t_dim // chunk_t, s_dim // CHUNK_S
    packed, padded = tables(rows, groups, ring)
    vmem = pl.BlockSpec(memory_space=pltpu.VMEM)
    anywhere = pl.BlockSpec(memory_space=pl.ANY)
    bf, f32 = jnp.bfloat16, jnp.float32
    dma = pltpu.SemaphoreType.DMA
    cube = (2, half, 2, line)
    loss, grads, hid, mine = pl.pallas_call(
        functools.partial(fused, rows, groups, ring),
        out_shape=(
            jax.ShapeDtypeStruct((1, tokens), f32),
            jax.ShapeDtypeStruct((tokens, vocab), bf),
            jax.ShapeDtypeStruct((n_s, tokens, CHUNK_S), bf),
            jax.ShapeDtypeStruct((n_s, pad, CHUNK_S), bf),
        ),
        in_specs=[vmem] * 6 + [anywhere] * 2,
        out_specs=(vmem, anywhere, anywhere, vmem),
        scratch_shapes=[
            pltpu.VMEM((n_t, *cube, block, chunk_t // FOLD), bf),
            pltpu.VMEM((n_s, *cube, block, CHUNK_S // FOLD), bf),
            pltpu.VMEM((SLOTS, chunk_t, vocab), bf),
            pltpu.VMEM((tokens, vocab), f32),
            pltpu.VMEM((tokens, vocab), f32),
            pltpu.VMEM((tokens, packed.shape[1]), bf),
            pltpu.VMEM((tokens, chunk_t), bf),
            pltpu.VMEM((n_s, tokens, CHUNK_S), bf),
            pltpu.VMEM((tokens, vocab), bf),
            pltpu.VMEM((devices * pad, tokens), bf),
            pltpu.VMEM((1, *cube, 8, tokens), f32),
            pltpu.VMEM((tokens, 128), f32),
            pltpu.VMEM((128, tokens), f32),
            pltpu.VMEM((tokens, 128), f32),
            pltpu.VMEM((n_s, *cube, pad, CHUNK_S), bf),
            pltpu.VMEM((n_s, half, 2, line, pad, CHUNK_S), bf),
            pltpu.VMEM((n_s, 2, mid, pad, CHUNK_S), bf),
            pltpu.VMEM((n_s, line - mid, pad, CHUNK_S), bf),
            pltpu.VMEM((n_s, mid, pad, CHUNK_S), bf),
            pltpu.VMEM((n_s, half, line - mid, pad, CHUNK_S), bf),
            pltpu.VMEM((n_s, line - 1, pad, CHUNK_S), bf),
            dma((SLOTS,)), dma((2,)),
            dma((n_t, line + 4)), dma((n_t, line + 4)),
            dma((n_s, line + 4)), dma((n_s, line + 4)),
            dma((1, line + 4)), dma((1, line + 4)),
            dma((n_s, line + 4)), dma((n_s, line + 4)),
        ],
        compiler_params=pltpu.CompilerParams(
            collective_id=0, has_side_effects=True, vmem_limit_bytes=62 * 2**20),
        cost_estimate=pl.CostEstimate(
            flops=2 * tokens * vocab * (t_dim + 2 * s_dim),
            bytes_accessed=2 * vocab * (t_dim + 2 * s_dim), transcendentals=4 * tokens * vocab),
    )(
        fold(teacher_hidden, chunk_t, block), fold(student_hidden, CHUNK_S, block),
        owner_map[:, None], labels[:, None], jnp.asarray(packed), jnp.asarray(padded),
        teacher_head, student_head,
    )
    grad_head = pl.pallas_call(
        head_kernel,
        out_shape=jax.ShapeDtypeStruct((s_dim, vocab), bf),
        grid=(n_s,),
        in_specs=[
            pl.BlockSpec((1, tokens, CHUNK_S), lambda i: (i, 0, 0)),
            pl.BlockSpec((tokens, vocab), lambda i: (0, 0)),
        ],
        out_specs=pl.BlockSpec((CHUNK_S, vocab), lambda i: (i, 0)),
        compiler_params=pltpu.CompilerParams(vmem_limit_bytes=40 * 2**20),
        cost_estimate=pl.CostEstimate(
            flops=2 * tokens * vocab * s_dim, bytes_accessed=2 * vocab * s_dim, transcendentals=0),
    )(hid, grads)
    position = lax.axis_index("grp") * ring + lax.axis_index("tp")
    token_loss = lax.dynamic_slice_in_dim(loss[0], position * rows, rows)
    grad_hidden = mine[:, :rows, :].transpose(1, 0, 2).reshape(rows, s_dim)
    return token_loss, grad_head, grad_hidden


def solution(mesh):
    groups, ring = mesh.shape["grp"], mesh.shape["tp"]
    in_specs = (
        P(("grp", "tp"), None),
        P(None, ("grp", "tp")),
        P(("grp", "tp"), None),
        P(None, ("grp", "tp")),
        P(),
        P(),
    )
    out_specs = (P(("grp", "tp")), P(None, ("grp", "tp")), P(("grp", "tp"), None))
    return jax.shard_map(
        functools.partial(shards, groups, ring),
        mesh=mesh, in_specs=in_specs, out_specs=out_specs, check_vma=False)
```
